32 devices in a mesh: req: 8 (over z, x), tp: 4 (over y, core).
Axes of the slice: x: 2, y: 2, z: 4, core: 2. Of those that a mesh axis runs over, the one named last changes fastest.
Arguments:
- queries: bfloat16 [64, 4096], P('req', 'tp'), may hold values from -320 to 320, as said below
- new_kv: bfloat16 [64, 2, 512], P('req', None, 'tp'), may hold values from -6 to 6
- own_kv: bfloat16 [64, 128, 2, 512], P('req', None, None, 'tp'), may hold values from -6 to 6
- prompt_kv: bfloat16 [8, 512, 2, 512], P('req', None, None, 'tp'), may hold values from -6 to 6
- out_weight: bfloat16 [4096, 2048], P('tp'), may hold values from -0.09375 to 0.09375
- parents: int32 [64], replicated, may hold values from 0 to 63, as said below
- own_len: int32 [64], replicated, may hold values from 1 to 128, as said below
- first_beam: int32 [64], replicated, may hold values from 0 to 63, as said below
Outputs:
- mixed_out: bfloat16 [64, 2048], P('req', 'tp')
The draws below stay inside these ranges and needn't reach their ends.
Inputs may be any that keep to these rules, and one draw needn't show every extreme that they name: Beams of one request are consecutive; first_beam[b] is the first of them; every request but the last holds 8 to 16 beams, and one holds exactly 16. parents[b] is a beam of the same request as b. `own_len`: some beam has exactly 128 valid positions. queries are real-valued, with row scales that may differ widely.
All inputs are finite; a program needn't handle non-finite values.
Results may differ from the reference program's by a relative error of at most 0.015.
Values may be sent and summed in bfloat16 or wider, within the bound.
A program may use at most 64 MiB of HBM per device.

```python
import jax
import jax.numpy as jnp
from jax import lax

H = 32
KVH = 4
HD = 128
W = 2048
BEAM_DEV = 8
MOST_BEAMS = 16
OWN_LEN = 128
PROMPT = 512
BEAMS = 64
HOMES = 8


def request_layout(key):
    request_count = BEAMS // BEAM_DEV + 1
    request_sizes = jax.random.randint(jax.random.fold_in(key, 11), (request_count,), BEAM_DEV, MOST_BEAMS + 1).astype(jnp.int32)
    request_sizes = request_sizes.at[0].set(MOST_BEAMS)
    request_ends = jnp.cumsum(request_sizes).astype(jnp.int32)
    request_starts = request_ends - request_sizes
    position = jnp.arange(BEAMS, dtype=jnp.int32)
    request_idx = jnp.sum((request_ends[None, :] <= position[:, None]).astype(jnp.int32), axis=1)
    first_slot = request_starts[request_idx]
    span_size = jnp.minimum(request_sizes[request_idx], BEAMS - first_slot)
    return (first_slot, span_size)


def draw_first_beam(key, part):
    return request_layout(key)[0]


def draw_parents(key, part):
    first_slot, span_size = request_layout(key)
    steps_drawn = jax.random.randint(jax.random.fold_in(key, 23), (BEAMS,), 0, span_size)
    chosen = (first_slot + steps_drawn).astype(jnp.int32)
    chosen = chosen.at[0].set(0)
    chosen = chosen.at[BEAMS - 1].set(BEAMS - 1)
    return chosen.astype(jnp.int32)


def draw_own_len(key, part):
    device_caps = jax.random.randint(jax.random.fold_in(key, 31), (BEAMS // BEAM_DEV,), max(OWN_LEN // 4, 1), OWN_LEN + 1)
    caps_beam = jnp.repeat(device_caps, BEAM_DEV)
    lengths = jax.random.randint(jax.random.fold_in(key, 37), (BEAMS,), 1, caps_beam + 1)
    return lengths.at[0].set(OWN_LEN).astype(jnp.int32)


def draw_queries(key, part):
    values_drawn = jax.random.truncated_normal(key, -4.0, 4.0, (BEAMS, H * HD), jnp.float32)
    return values_drawn.astype(jnp.bfloat16)


def shard_levels(own_key, extent, shards, smallest, high):
    factor_of = 1.0
    for axis_at, shards_of in shards:
        draws = jax.random.uniform(jax.random.fold_in(jax.random.fold_in(own_key, 6), axis_at), (shards_of,), jnp.float32, smallest / len(shards), high / len(shards))
        factor_of = factor_of * jnp.repeat(jnp.exp(draws), extent[axis_at] // shards_of).reshape((-1,) + (1,) * (len(extent) - 1 - axis_at))
    return factor_of


def scatter_about(own_key, shape, width, bound, pieces=(), kind=jnp.bfloat16):
    values = width * jax.random.normal(own_key, shape, jnp.float32)
    if pieces:
        values = values * shard_levels(own_key, shape, pieces, -0.22, 0.18)
    return jnp.clip(values, -bound, bound).astype(kind)


def setup_inputs(seed: int = 0) -> dict:
    seeds = jax.random.split(jax.random.key(seed), 9)
    return {
        "queries": draw_queries(jax.random.fold_in(seeds[8], 71), 0),
        "new_kv": scatter_about(seeds[1], (BEAMS, 2, KVH * HD), 1.0, 6.0, ((0, 8), (2, 4))),
        "own_kv": scatter_about(seeds[2], (BEAMS, OWN_LEN, 2, KVH * HD), 1.0, 6.0, ((0, 8), (3, 4))),
        "prompt_kv": scatter_about(seeds[3], (HOMES, PROMPT, 2, KVH * HD), 1.0, 6.0, ((0, 8), (3, 4))),
        "out_weight": scatter_about(seeds[4], (H * HD, W), (H * HD) ** -0.5, 0.09375, ((0, 4),)),
        "parents": draw_parents(jax.random.fold_in(seeds[8], 71), 0),
        "own_len": draw_own_len(jax.random.fold_in(seeds[8], 71), 0),
        "first_beam": draw_first_beam(jax.random.fold_in(seeds[8], 71), 0),
    }


def reference(queries, new_kv, own_kv, prompt_kv, out_weight, parents, own_len, first_beam):
    score_scale = HD ** -0.5
    home_slots = (first_beam // BEAM_DEV).astype(jnp.int32)
    own_positions = jnp.arange(OWN_LEN, dtype=jnp.int32)

    def attend_beam(entries):
        query_row, parent, home_slot, fresh_row = entries
        key_rows = jnp.concatenate([prompt_kv[home_slot], own_kv[parent], fresh_row[None]], axis=0)
        allowed = jnp.concatenate([jnp.ones((PROMPT,), bool), own_positions < own_len[parent], jnp.ones((1,), bool)])
        keys_f = key_rows[:, 0].astype(jnp.float32).reshape(-1, KVH, HD)
        values_f = key_rows[:, 1].astype(jnp.float32).reshape(-1, KVH, HD)
        query_heads = query_row.astype(jnp.float32).reshape(KVH, H // KVH, HD)
        scores = jnp.einsum("kgd,skd->kgs", query_heads, keys_f, precision=lax.Precision.HIGHEST) * score_scale
        scores = jnp.where(allowed, scores, -1.0e30)
        weights = jax.nn.softmax(scores, axis=-1)
        attended = jnp.einsum("kgs,skd->kgd", weights, values_f, precision=lax.Precision.HIGHEST)
        return attended.reshape(H * HD).astype(jnp.bfloat16)

    attended_all = lax.map(attend_beam, (queries, parents, home_slots, new_kv))
    return jnp.dot(attended_all, out_weight, preferred_element_type=jnp.float32).astype(jnp.bfloat16)
```

```python
import functools

import jax
import jax.numpy as jnp
from jax import lax
from jax.experimental import pallas as pl
from jax.experimental.pallas import tpu as pltpu
from jax.sharding import PartitionSpec as P

HD = 128
MOST_BEAMS = 16
NEG = -1e30
MESH = pl.DeviceIdType.MESH

NEAR = (1, 2, -1, -2)


def nt(a, b):
    return lax.dot_general(
        a, b, (((1,), (1,)), ((), ())), preferred_element_type=jnp.float32
    )


def kernel(
    n, n_tp,
    q_ref, new_ref, own_hbm, prompt_hbm, w_hbm, parents, own_len, first_beam,
    out_ref,
    qs, qin, kvb, kvf, newf, kb, vb, wv, res, rin, part, pin,
    load_sem, q_send, q_recv, r_send, r_recv, o_send, o_recv,
):
    per_dev = q_ref.shape[0]
    groups = q_ref.shape[1] // HD
    rows = per_dev * groups
    own_rows, prompt_rows = own_hbm.shape[0], prompt_hbm.shape[0]
    n_own, n_prompt = own_rows // 2, prompt_rows // 2
    n_keys = n_own + n_prompt
    cache = n_own // per_dev
    scale = HD ** -0.5
    d = lax.axis_index("req")
    t = lax.axis_index("tp")

    def there(delta):
        return d + delta < n if delta > 0 else d + delta >= 0

    own_load = pltpu.make_async_copy(own_hbm, kvb.at[pl.ds(0, own_rows)], load_sem.at[0])
    prompt_load = pltpu.make_async_copy(
        prompt_hbm, kvb.at[pl.ds(own_rows, prompt_rows)], load_sem.at[1]
    )
    w_load = pltpu.make_async_copy(w_hbm, wv, load_sem.at[2])

    barrier = pltpu.get_barrier_semaphore()
    for delta in NEAR:
        @pl.when(there(delta))
        def _():
            pl.semaphore_signal(
                barrier, inc=1, device_id={"req": d + delta}, device_id_type=MESH
            )
    for j in range(1, n_tp):
        pl.semaphore_signal(
            barrier, inc=1, device_id={"tp": lax.rem(t + j, n_tp)}, device_id_type=MESH
        )
    own_load.start()
    prompt_load.start()
    w_load.start()

    qf = q_ref[...].astype(jnp.float32)
    qrows = jnp.concatenate([qf[:, g * HD:(g + 1) * HD] for g in range(groups)], axis=0)
    qs[...] = qrows.astype(jnp.bfloat16)

    for k, delta in enumerate(NEAR):
        @pl.when(jnp.logical_not(there(delta)))
        def _():
            qin[pl.ds(k * rows, rows), :] = jnp.zeros((rows, HD), jnp.bfloat16)
            rin[k] = jnp.zeros(rin.shape[1:], jnp.bfloat16)

    peers = n_tp - 1
    for delta in NEAR:
        peers = peers + jnp.where(there(delta), 1, 0)
    pl.semaphore_wait(barrier, peers)

    def q_copy(k, target):
        return pltpu.make_async_remote_copy(
            src_ref=qs,
            dst_ref=qin.at[pl.ds(k * rows, rows)],
            send_sem=q_send.at[k],
            recv_sem=q_recv.at[k],
            device_id={"req": target},
            device_id_type=MESH,
        )

    def r_copy(k_from, k_to, target):
        return pltpu.make_async_remote_copy(
            src_ref=res.at[k_from],
            dst_ref=rin.at[k_to],
            send_sem=r_send.at[k_to],
            recv_sem=r_recv.at[k_to],
            device_id={"req": target},
            device_id_type=MESH,
        )

    for delta in NEAR:
        @pl.when(there(delta))
        def _():
            q_copy(NEAR.index(-delta), d + delta).start()

    sub = lax.broadcasted_iota(jnp.int32, (per_dev, HD), 0)
    lane = lax.broadcasted_iota(jnp.int32, (per_dev, HD), 1)

    def beam_facts(delta):
        source = lax.rem(d + delta + n, n)
        rel = jnp.zeros((per_dev, HD), jnp.int32)
        length = jnp.zeros((per_dev, HD), jnp.int32)
        gap = jnp.zeros((per_dev, HD), jnp.int32)
        for i in range(per_dev):
            b = source * per_dev + i
            parent = parents[b]
            here = sub == i
            rel = jnp.where(here, parent - d * per_dev, rel)
            length = jnp.where(here, own_len[parent], length)
            if delta >= 0:
                gap = jnp.where(here, first_beam[b] - d * per_dev, gap)
        return rel, length, gap

    facts = {delta: beam_facts(delta) for delta in (0,) + NEAR}

    def spread(deltas, which):
        return jnp.concatenate(
            [facts[delta][which] for delta in deltas for _ in range(groups)], axis=0
        )

    newf[...] = new_ref[...].astype(jnp.float32)
    new_k = newf[pl.ds(0, per_dev, stride=2), :]
    new_v = newf[pl.ds(1, per_dev, stride=2), :]

    own_load.wait()
    kvf[pl.ds(0, own_rows), :] = kvb[pl.ds(0, own_rows), :].astype(jnp.float32)
    prompt_load.wait()
    kvf[pl.ds(own_rows, prompt_rows), :] = kvb[pl.ds(own_rows, prompt_rows), :].astype(jnp.float32)
    kb[...] = kvf[pl.ds(0, n_keys, stride=2), :].astype(jnp.bfloat16)
    vb[...] = kvf[pl.ds(1, n_keys, stride=2), :].astype(jnp.bfloat16)

    def attend(q, deltas, fresh=None):
        rel = spread(deltas, 0)
        length = spread(deltas, 1)
        lanes = lax.broadcasted_iota(jnp.int32, rel.shape, 1)
        s = jnp.full(rel.shape, NEG, jnp.float32)
        for c in range(per_dev):
            s = jnp.where(rel == c, nt(q, kb[pl.ds(c * cache, cache), :]), s)
        s = jnp.where(lanes < length, s, NEG)
        prompt = []
        if min(deltas) >= 0:
            gap = spread(deltas, 2)
            mine = (gap >= 0) & (gap < per_dev)
            for c in range(n_prompt // HD):
                sp = nt(q, kb[pl.ds(n_own + c * HD, HD), :])
                prompt.append(jnp.where(mine, sp, NEG))
        top = functools.reduce(jnp.maximum, prompt, s)
        m = jnp.max(top, axis=1, keepdims=True)
        if fresh is not None:
            m = jnp.maximum(m, fresh)
        p = jnp.exp((s - m) * scale)
        weights = [jnp.exp((sp - m) * scale).astype(jnp.bfloat16) for sp in prompt]
        total = functools.reduce(
            jnp.add,
            [x.astype(jnp.float32) for x in weights],
            p.astype(jnp.bfloat16).astype(jnp.float32),
        )
        total = jnp.sum(total, axis=1, keepdims=True)
        picked = [jnp.where(rel == c, p, 0.0).astype(jnp.bfloat16) for c in range(per_dev)]
        table = jnp.concatenate(picked + weights, axis=1)
        w = jnp.dot(table, vb[pl.ds(0, table.shape[1]), :], preferred_element_type=jnp.float32)
        return m, total, w

    k_tiled = jnp.concatenate([new_k] * groups, axis=0)
    v_tiled = jnp.concatenate([new_v] * groups, axis=0)
    fresh = jnp.sum(qrows * k_tiled, axis=1, keepdims=True)
    m0, l0, w0 = attend(qs[...], (0,), fresh)
    pf = jnp.exp((fresh - m0) * scale)
    l0 = l0 + pf
    w0 = w0 + pf * v_tiled

    for pair in (0, 1):
        deltas = NEAR[2 * pair:2 * pair + 2]
        for k in (2 * pair, 2 * pair + 1):
            @pl.when(there(NEAR[k]))
            def _():
                q_copy(k, d + NEAR[k]).wait_recv()
        m, total, w = attend(qin[pl.ds(2 * pair * rows, 2 * rows), :], deltas)
        lanes = lax.broadcasted_iota(jnp.int32, w.shape, 1)
        stats = jnp.zeros(w.shape, jnp.float32)
        at = 0
        for value, count in ((m, 3), (total, 2)):
            left = value
            for _ in range(count):
                piece = left.astype(jnp.bfloat16).astype(jnp.float32)
                left = left - piece
                stats = jnp.where(lanes == at, piece, stats)
                at += 1
        for i in (0, 1):
            k = 2 * pair + i
            res[k, :, pl.ds(0, HD)] = w[i * rows:(i + 1) * rows].astype(jnp.bfloat16)
            res[k, :, pl.ds(HD, HD)] = stats[i * rows:(i + 1) * rows].astype(jnp.bfloat16)
            @pl.when(there(NEAR[k]))
            def _():
                r_copy(k, NEAR.index(-NEAR[k]), d + NEAR[k]).start()

    parts = [(m0, l0, w0)]
    for k, delta in enumerate(NEAR):
        @pl.when(there(delta))
        def _():
            r_copy(k, k, d + delta).wait_recv()
        w = rin[k, :, pl.ds(0, HD)].astype(jnp.float32)
        st = rin[k, :, pl.ds(HD, HD)].astype(jnp.float32)
        m = st[:, 0:1] + st[:, 1:2] + st[:, 2:3]
        l = st[:, 3:4] + st[:, 4:5]
        m = jnp.where(there(delta), m, NEG)
        parts.append((m, l, w))
    peak = functools.reduce(jnp.maximum, [x[0] for x in parts])
    weighted = jnp.zeros((rows, HD), jnp.float32)
    total = jnp.zeros((rows, 1), jnp.float32)
    for m, l, w in parts:
        f = jnp.exp((m - peak) * scale)
        weighted = weighted + w * f
        total = total + l * f
    att = weighted / total
    att = jnp.concatenate(
        [att[g * per_dev:(g + 1) * per_dev] for g in range(groups)], axis=1
    ).astype(jnp.bfloat16)

    w_load.wait()
    width = w_hbm.shape[1] // n_tp

    def o_copy(j):
        return pltpu.make_async_remote_copy(
            src_ref=part.at[j - 1],
            dst_ref=pin.at[j - 1],
            send_sem=o_send.at[j - 1],
            recv_sem=o_recv.at[j - 1],
            device_id={"tp": lax.rem(t + j, n_tp)},
            device_id_type=MESH,
        )

    def project(j):
        start = pl.multiple_of(lax.rem(t + j, n_tp) * width, width)
        y = jnp.dot(att, wv[:, pl.ds(start, width)], preferred_element_type=jnp.float32)
        return jnp.concatenate([y[:, :width // 2], y[:, width // 2:]], axis=0)

    for j in range(n_tp - 1, 0, -1):
        part[j - 1] = project(j).astype(jnp.bfloat16)
        o_copy(j).start()
    y = project(0)
    for j in range(n_tp - 1, 0, -1):
        o_copy(j).wait_recv()
        y = y + pin[j - 1].astype(jnp.float32)
    y = jnp.concatenate([y[:per_dev], y[per_dev:]], axis=1)
    out_ref[...] = y.astype(jnp.bfloat16)

    for k, delta in enumerate(NEAR):
        @pl.when(there(delta))
        def _():
            q_copy(NEAR.index(-delta), d + delta).wait_send()
            r_copy(k, NEAR.index(-delta), d + delta).wait_send()
    for j in range(1, n_tp):
        o_copy(j).wait_send()


def local(n, n_tp, queries, new_kv, own_kv, prompt_kv, out_weight, parents, own_len, first_beam):
    per_dev, q_width = queries.shape
    rows = per_dev * q_width // HD
    own = own_kv.reshape(-1, HD)
    prompt = prompt_kv.reshape(-1, HD)
    new = new_kv.reshape(-1, HD)
    total = own.shape[0] + prompt.shape[0]
    width = out_weight.shape[1] // n_tp
    vmem = pl.BlockSpec(memory_space=pltpu.VMEM)
    smem = pl.BlockSpec(memory_space=pltpu.SMEM)
    hbm = pl.BlockSpec(memory_space=pl.ANY)
    near = len(NEAR)
    bf16, f32 = jnp.bfloat16, jnp.float32
    dma = pltpu.SemaphoreType.DMA
    return pl.pallas_call(
        functools.partial(kernel, n, n_tp),
        out_shape=jax.ShapeDtypeStruct((per_dev, width), bf16),
        in_specs=[vmem, vmem, hbm, hbm, hbm, smem, smem, smem],
        out_specs=vmem,
        scratch_shapes=[
            pltpu.VMEM((rows, HD), bf16),
            pltpu.VMEM((near * rows, HD), bf16),
            pltpu.VMEM((total, HD), bf16),
            pltpu.VMEM((total, HD), f32),
            pltpu.VMEM(new.shape, f32),
            pltpu.VMEM((total // 2, HD), bf16),
            pltpu.VMEM((total // 2, HD), bf16),
            pltpu.VMEM(out_weight.shape, bf16),
            pltpu.VMEM((near, rows, 2 * HD), bf16),
            pltpu.VMEM((near, rows, 2 * HD), bf16),
            pltpu.VMEM((n_tp - 1, 2 * per_dev, width // 2), bf16),
            pltpu.VMEM((n_tp - 1, 2 * per_dev, width // 2), bf16),
            dma((3,)),
            dma((near,)),
            dma((near,)),
            dma((near,)),
            dma((near,)),
            dma((n_tp - 1,)),
            dma((n_tp - 1,)),
        ],
        compiler_params=pltpu.CompilerParams(
            collective_id=0, has_side_effects=True, vmem_limit_bytes=48 * 1024 * 1024
        ),
    )(queries, new, own, prompt, out_weight, parents, own_len, first_beam)


def solution(mesh):
    in_specs = (
        P("req", "tp"),
        P("req", None, "tp"),
        P("req", None, None, "tp"),
        P("req", None, None, "tp"),
        P("tp", None),
        P(),
        P(),
        P(),
    )
    out_specs = P("req", "tp")
    run = functools.partial(local, mesh.shape["req"], mesh.shape["tp"])
    return jax.shard_map(run, mesh=mesh, in_specs=in_specs, out_specs=out_specs, check_vma=False)
```

```python
import functools

import jax
import jax.numpy as jnp
from jax import lax
from jax.experimental import pallas as pl
from jax.experimental.pallas import tpu as pltpu
from jax.sharding import PartitionSpec as P

HD = 128
MOST_BEAMS = 16
NEG = -1e30
MESH = pl.DeviceIdType.MESH

NEAR = (1, 2, -1, -2)


def nt(a, b):
    return lax.dot_general(
        a, b, (((1,), (1,)), ((), ())), preferred_element_type=jnp.float32
    )


def kernel(
    n, n_tp,
    q_ref, new_ref, own_hbm, prompt_hbm, w_hbm, parents, own_len, first_beam,
    out_ref,
    qs, qin, kvb, kvf, newf, kb, vb, wv, res, rin, part, pin,
    load_sem, q_send, q_recv, r_send, r_recv, o_send, o_recv,
):
    per_dev = q_ref.shape[0]
    groups = q_ref.shape[1] // HD
    rows = per_dev * groups
    own_rows, prompt_rows = own_hbm.shape[0], prompt_hbm.shape[0]
    n_own, n_prompt = own_rows // 2, prompt_rows // 2
    n_keys = n_own + n_prompt
    cache = n_own // per_dev
    scale = HD ** -0.5
    d = lax.axis_index("req")
    t = lax.axis_index("tp")

    def there(delta):
        return d + delta < n if delta > 0 else d + delta >= 0

    own_load = pltpu.make_async_copy(own_hbm, kvb.at[pl.ds(0, own_rows)], load_sem.at[0])
    prompt_load = pltpu.make_async_copy(
        prompt_hbm, kvb.at[pl.ds(own_rows, prompt_rows)], load_sem.at[1]
    )
    w_load = pltpu.make_async_copy(w_hbm, wv, load_sem.at[2])

    barrier = pltpu.get_barrier_semaphore()
    for delta in NEAR:
        @pl.when(there(delta))
        def _():
            pl.semaphore_signal(
                barrier, inc=1, device_id={"req": d + delta}, device_id_type=MESH
            )
    for j in range(1, n_tp):
        pl.semaphore_signal(
            barrier, inc=1, device_id={"tp": lax.rem(t + j, n_tp)}, device_id_type=MESH
        )
    own_load.start()
    prompt_load.start()
    w_load.start()

    qf = q_ref[...].astype(jnp.float32)
    qrows = jnp.concatenate([qf[:, g * HD:(g + 1) * HD] for g in range(groups)], axis=0)
    qs[...] = qrows.astype(jnp.bfloat16)

    for k, delta in enumerate(NEAR):
        @pl.when(jnp.logical_not(there(delta)))
        def _():
            qin[pl.ds(k * rows, rows), :] = jnp.zeros((rows, HD), jnp.bfloat16)
            rin[k] = jnp.zeros(rin.shape[1:], jnp.bfloat16)

    peers = n_tp - 1
    for delta in NEAR:
        peers = peers + jnp.where(there(delta), 1, 0)
    pl.semaphore_wait(barrier, peers)

    def q_copy(k, target):
        return pltpu.make_async_remote_copy(
            src_ref=qs,
            dst_ref=qin.at[pl.ds(k * rows, rows)],
            send_sem=q_send.at[k],
            recv_sem=q_recv.at[k],
            device_id={"req": target},
            device_id_type=MESH,
        )

    def r_copy(k_from, k_to, target):
        return pltpu.make_async_remote_copy(
            src_ref=res.at[k_from],
            dst_ref=rin.at[k_to],
            send_sem=r_send.at[k_to],
            recv_sem=r_recv.at[k_to],
            device_id={"req": target},
            device_id_type=MESH,
        )

    for delta in NEAR:
        @pl.when(there(delta))
        def _():
            q_copy(NEAR.index(-delta), d + delta).start()

    sub = lax.broadcasted_iota(jnp.int32, (per_dev, HD), 0)
    lane = lax.broadcasted_iota(jnp.int32, (per_dev, HD), 1)

    def beam_facts(delta):
        source = lax.rem(d + delta + n, n)
        rel = jnp.zeros((per_dev, HD), jnp.int32)
        length = jnp.zeros((per_dev, HD), jnp.int32)
        gap = jnp.zeros((per_dev, HD), jnp.int32)
        for i in range(per_dev):
            b = source * per_dev + i
            parent = parents[b]
            here = sub == i
            rel = jnp.where(here, parent - d * per_dev, rel)
            length = jnp.where(here, own_len[parent], length)
            if delta >= 0:
                gap = jnp.where(here, first_beam[b] - d * per_dev, gap)
        return rel, length, gap

    facts = {delta: beam_facts(delta) for delta in (0,) + NEAR}

    def spread(deltas, which):
        return jnp.concatenate(
            [facts[delta][which] for delta in deltas for _ in range(groups)], axis=0
        )

    newf[...] = new_ref[...].astype(jnp.float32)
    new_k = newf[pl.ds(0, per_dev, stride=2), :]
    new_v = newf[pl.ds(1, per_dev, stride=2), :]

    own_load.wait()
    kvf[pl.ds(0, own_rows), :] = kvb[pl.ds(0, own_rows), :].astype(jnp.float32)
    prompt_load.wait()
    kvf[pl.ds(own_rows, prompt_rows), :] = kvb[pl.ds(own_rows, prompt_rows), :].astype(jnp.float32)
    kb[...] = kvf[pl.ds(0, n_keys, stride=2), :].astype(jnp.bfloat16)
    vb[...] = kvf[pl.ds(1, n_keys, stride=2), :].astype(jnp.bfloat16)

    def attend(q, deltas, fresh=None):
        rel = spread(deltas, 0)
        length = spread(deltas, 1)
        lanes = lax.broadcasted_iota(jnp.int32, rel.shape, 1)
        s = jnp.full(rel.shape, NEG, jnp.float32)
        for c in range(per_dev):
            s = jnp.where(rel == c, nt(q, kb[pl.ds(c * cache, cache), :]), s)
        s = jnp.where(lanes < length, s, NEG)
        prompt = []
        if min(deltas) >= 0:
            gap = spread(deltas, 2)
            mine = (gap >= 0) & (gap < per_dev)
            for c in range(n_prompt // HD):
                sp = nt(q, kb[pl.ds(n_own + c * HD, HD), :])
                prompt.append(jnp.where(mine, sp, NEG))
        top = functools.reduce(jnp.maximum, prompt, s)
        m = jnp.max(top, axis=1, keepdims=True)
        if fresh is not None:
            m = jnp.maximum(m, fresh)
        p = jnp.exp((s - m) * scale)
        weights = [jnp.exp((sp - m) * scale).astype(jnp.bfloat16) for sp in prompt]
        total = functools.reduce(
            jnp.add,
            [x.astype(jnp.float32) for x in weights],
            p.astype(jnp.bfloat16).astype(jnp.float32),
        )
        total = jnp.sum(total, axis=1, keepdims=True)
        picked = [jnp.where(rel == c, p, 0.0).astype(jnp.bfloat16) for c in range(per_dev)]
        table = jnp.concatenate(picked + weights, axis=1)
        w = jnp.dot(table, vb[pl.ds(0, table.shape[1]), :], preferred_element_type=jnp.float32)
        return m, total, w

    k_tiled = jnp.concatenate([new_k] * groups, axis=0)
    v_tiled = jnp.concatenate([new_v] * groups, axis=0)
    fresh = jnp.sum(qrows * k_tiled, axis=1, keepdims=True)
    m0, l0, w0 = attend(qs[...], (0,), fresh)
    pf = jnp.exp((fresh - m0) * scale)
    l0 = l0 + pf
    w0 = w0 + pf * v_tiled

    for pair in (0, 1):
        deltas = NEAR[2 * pair:2 * pair + 2]
        for k in (2 * pair, 2 * pair + 1):
            @pl.when(there(NEAR[k]))
            def _():
                q_copy(k, d + NEAR[k]).wait_recv()
        m, total, w = attend(qin[pl.ds(2 * pair * rows, 2 * rows), :], deltas)
        lanes = lax.broadcasted_iota(jnp.int32, w.shape, 1)
        stats = jnp.zeros(w.shape, jnp.float32)
        at = 0
        for value, count in ((m, 3), (total, 2)):
            left = value
            for _ in range(count):
                piece = left.astype(jnp.bfloat16).astype(jnp.float32)
                left = left - piece
                stats = jnp.where(lanes == at, piece, stats)
                at += 1
        for i in (0, 1):
            k = 2 * pair + i
            res[k, :, pl.ds(0, HD)] = w[i * rows:(i + 1) * rows].astype(jnp.bfloat16)
            res[k, :, pl.ds(HD, HD)] = stats[i * rows:(i + 1) * rows].astype(jnp.bfloat16)
            @pl.when(there(NEAR[k]))
            def _():
                r_copy(k, NEAR.index(-NEAR[k]), d + NEAR[k]).start()

    parts = [(m0, l0, w0)]
    for k, delta in enumerate(NEAR):
        @pl.when(there(delta))
        def _():
            r_copy(k, k, d + delta).wait_recv()
        w = rin[k, :, pl.ds(0, HD)].astype(jnp.float32)
        st = rin[k, :, pl.ds(HD, HD)].astype(jnp.float32)
        m = st[:, 0:1] + st[:, 1:2] + st[:, 2:3]
        l = st[:, 3:4] + st[:, 4:5]
        m = jnp.where(there(delta), m, NEG)
        parts.append((m, l, w))
    peak = functools.reduce(jnp.maximum, [x[0] for x in parts])
    weighted = jnp.zeros((rows, HD), jnp.float32)
    total = jnp.zeros((rows, 1), jnp.float32)
    for m, l, w in parts:
        f = jnp.exp((m - peak) * scale)
        weighted = weighted + w * f
        total = total + l * f
    att = weighted / total
    att = jnp.concatenate(
        [att[g * per_dev:(g + 1) * per_dev] for g in range(groups)], axis=1
    ).astype(jnp.bfloat16)

    w_load.wait()
    width = w_hbm.shape[1] // n_tp

    def o_copy(j):
        return pltpu.make_async_remote_copy(
            src_ref=part.at[j - 1],
            dst_ref=pin.at[j - 1],
            send_sem=o_send.at[j - 1],
            recv_sem=o_recv.at[j - 1],
            device_id={"tp": lax.rem(t + j, n_tp)},
            device_id_type=MESH,
        )

    def project(j):
        start = pl.multiple_of(lax.rem(t + j, n_tp) * width, width)
        y = jnp.dot(att, wv[:, pl.ds(start, width)], preferred_element_type=jnp.float32)
        return jnp.concatenate([y[:, :width // 2], y[:, width // 2:]], axis=0)

    for j in range(n_tp - 1, 0, -1):
        part[j - 1] = project(j).astype(jnp.bfloat16)
        o_copy(j).start()
    y = project(0)
    for j in range(n_tp - 1, 0, -1):
        o_copy(j).wait_recv()
        y = y + pin[j - 1].astype(jnp.float32)
    y = jnp.concatenate([y[:per_dev], y[per_dev:]], axis=1)
    out_ref[...] = y.astype(jnp.bfloat16)

    for k, delta in enumerate(NEAR):
        @pl.when(there(delta))
        def _():
            q_copy(NEAR.index(-delta), d + delta).wait_send()
            r_copy(k, NEAR.index(-delta), d + delta).wait_send()
    for j in range(1, n_tp):
        o_copy(j).wait_send()


def local(n, n_tp, queries, new_kv, own_kv, prompt_kv, out_weight, parents, own_len, first_beam):
    per_dev, q_width = queries.shape
    rows = per_dev * q_width // HD
    own = own_kv.reshape(-1, HD)
    prompt = prompt_kv.reshape(-1, HD)
    new = new_kv.reshape(-1, HD)
    total = own.shape[0] + prompt.shape[0]
    width = out_weight.shape[1] // n_tp
    vmem = pl.BlockSpec(memory_space=pltpu.VMEM)
    smem = pl.BlockSpec(memory_space=pltpu.SMEM)
    hbm = pl.BlockSpec(memory_space=pl.ANY)
    near = len(NEAR)
    bf16, f32 = jnp.bfloat16, jnp.float32
    dma = pltpu.SemaphoreType.DMA
    return pl.pallas_call(
        functools.partial(kernel, n, n_tp),
        out_shape=jax.ShapeDtypeStruct((per_dev, width), bf16),
        in_specs=[vmem, vmem, hbm, hbm, hbm, smem, smem, smem],
        out_specs=vmem,
        scratch_shapes=[
            pltpu.VMEM((rows, HD), bf16),
            pltpu.VMEM((near * rows, HD), bf16),
            pltpu.VMEM((total, HD), bf16),
            pltpu.VMEM((total, HD), f32),
            pltpu.VMEM(new.shape, f32),
            pltpu.VMEM((total // 2, HD), bf16),
            pltpu.VMEM((total // 2, HD), bf16),
            pltpu.VMEM(out_weight.shape, bf16),
            pltpu.VMEM((near, rows, 2 * HD), bf16),
            pltpu.VMEM((near, rows, 2 * HD), bf16),
            pltpu.VMEM((n_tp - 1, 2 * per_dev, width // 2), bf16),
            pltpu.VMEM((n_tp - 1, 2 * per_dev, width // 2), bf16),
            dma((3,)),
            dma((near,)),
            dma((near,)),
            dma((near,)),
            dma((near,)),
            dma((n_tp - 1,)),
            dma((n_tp - 1,)),
        ],
        compiler_params=pltpu.CompilerParams(
            collective_id=0, has_side_effects=True, vmem_limit_bytes=58 * 1024 * 1024
        ),
    )(queries, new, own, prompt, out_weight, parents, own_len, first_beam)


def solution(mesh):
    in_specs = (
        P("req", "tp"),
        P("req", None, "tp"),
        P("req", None, None, "tp"),
        P("req", None, None, "tp"),
        P("tp", None),
        P(),
        P(),
        P(),
    )
    out_specs = P("req", "tp")
    run = functools.partial(local, mesh.shape["req"], mesh.shape["tp"])
    return jax.shard_map(run, mesh=mesh, in_specs=in_specs, out_specs=out_specs, check_vma=False)
```

```python
import functools

import jax
import jax.numpy as jnp
from jax import lax
from jax.experimental import pallas as pl
from jax.experimental.pallas import tpu as pltpu
from jax.sharding import PartitionSpec as P

HD = 128
MOST_BEAMS = 16
NEG = -1e30
MESH = pl.DeviceIdType.MESH

NEAR = (1, 2, -1, -2)


def nt(a, b):
    return lax.dot_general(
        a, b, (((1,), (1,)), ((), ())), preferred_element_type=jnp.float32
    )


def kernel(
    n, n_tp,
    q_ref, new_ref, own_hbm, prompt_hbm, w_hbm, parents, own_len, first_beam,
    out_ref,
    qs, qin, kvb, kvf, newf, kb, vb, wv, res, rin, part, pin,
    load_sem, q_send, q_recv, r_send, r_recv, o_send, o_recv,
):
    per_dev = q_ref.shape[0]
    groups = q_ref.shape[1] // HD
    rows = per_dev * groups
    own_rows, prompt_rows = own_hbm.shape[0], prompt_hbm.shape[0]
    n_own, n_prompt = own_rows // 2, prompt_rows // 2
    n_keys = n_own + n_prompt
    cache = n_own // per_dev
    scale = HD ** -0.5
    d = lax.axis_index("req")
    t = lax.axis_index("tp")

    def there(delta):
        return d + delta < n if delta > 0 else d + delta >= 0

    own_load = pltpu.make_async_copy(own_hbm, kvb.at[pl.ds(0, own_rows)], load_sem.at[0])
    prompt_load = pltpu.make_async_copy(
        prompt_hbm, kvb.at[pl.ds(own_rows, prompt_rows)], load_sem.at[1]
    )
    w_load = pltpu.make_async_copy(w_hbm, wv, load_sem.at[2])

    barrier = pltpu.get_barrier_semaphore()
    for delta in NEAR:
        @pl.when(there(delta))
        def _():
            pl.semaphore_signal(
                barrier, inc=1, device_id={"req": d + delta}, device_id_type=MESH
            )
    for j in range(1, n_tp):
        pl.semaphore_signal(
            barrier, inc=1, device_id={"tp": lax.rem(t + j, n_tp)}, device_id_type=MESH
        )
    own_load.start()
    prompt_load.start()
    w_load.start()

    qf = q_ref[...].astype(jnp.float32)
    qrows = jnp.concatenate([qf[:, g * HD:(g + 1) * HD] for g in range(groups)], axis=0)
    qs[...] = qrows.astype(jnp.bfloat16)

    for k, delta in enumerate(NEAR):
        @pl.when(jnp.logical_not(there(delta)))
        def _():
            qin[pl.ds(k * rows, rows), :] = jnp.zeros((rows, HD), jnp.bfloat16)
            rin[k] = jnp.zeros(rin.shape[1:], jnp.bfloat16)

    peers = n_tp - 1
    for delta in NEAR:
        peers = peers + jnp.where(there(delta), 1, 0)
    pl.semaphore_wait(barrier, peers)

    def q_copy(k, target):
        return pltpu.make_async_remote_copy(
            src_ref=qs,
            dst_ref=qin.at[pl.ds(k * rows, rows)],
            send_sem=q_send.at[k],
            recv_sem=q_recv.at[k],
            device_id={"req": target},
            device_id_type=MESH,
        )

    def r_copy(k_from, k_to, target):
        return pltpu.make_async_remote_copy(
            src_ref=res.at[k_from],
            dst_ref=rin.at[k_to],
            send_sem=r_send.at[k_to],
            recv_sem=r_recv.at[k_to],
            device_id={"req": target},
            device_id_type=MESH,
        )

    for delta in NEAR:
        @pl.when(there(delta))
        def _():
            q_copy(NEAR.index(-delta), d + delta).start()

    sub = lax.broadcasted_iota(jnp.int32, (per_dev, HD), 0)
    lane = lax.broadcasted_iota(jnp.int32, (per_dev, HD), 1)

    def beam_facts(delta):
        source = lax.rem(d + delta + n, n)
        rel = jnp.zeros((per_dev, HD), jnp.int32)
        length = jnp.zeros((per_dev, HD), jnp.int32)
        gap = jnp.zeros((per_dev, HD), jnp.int32)
        for i in range(per_dev):
            b = source * per_dev + i
            parent = parents[b]
            here = sub == i
            rel = jnp.where(here, parent - d * per_dev, rel)
            length = jnp.where(here, own_len[parent], length)
            if delta >= 0:
                gap = jnp.where(here, first_beam[b] - d * per_dev, gap)
        return rel, length, gap

    facts = {delta: beam_facts(delta) for delta in (0,) + NEAR}

    def spread(deltas, which):
        return jnp.concatenate(
            [facts[delta][which] for delta in deltas for _ in range(groups)], axis=0
        )

    newf[...] = new_ref[...].astype(jnp.float32)
    new_k = newf[pl.ds(0, per_dev, stride=2), :]
    new_v = newf[pl.ds(1, per_dev, stride=2), :]

    own_load.wait()
    kvf[pl.ds(0, own_rows), :] = kvb[pl.ds(0, own_rows), :].astype(jnp.float32)
    prompt_load.wait()
    kvf[pl.ds(own_rows, prompt_rows), :] = kvb[pl.ds(own_rows, prompt_rows), :].astype(jnp.float32)
    kb[...] = kvf[pl.ds(0, n_keys, stride=2), :].astype(jnp.bfloat16)
    vb[...] = kvf[pl.ds(1, n_keys, stride=2), :].astype(jnp.bfloat16)

    def attend(q, deltas, fresh=None):
        rel = spread(deltas, 0)
        length = spread(deltas, 1)
        lanes = lax.broadcasted_iota(jnp.int32, rel.shape, 1)
        s = jnp.full(rel.shape, NEG, jnp.float32)
        for c in range(per_dev):
            s = jnp.where(rel == c, nt(q, kb[pl.ds(c * cache, cache), :]), s)
        s = jnp.where(lanes < length, s, NEG)
        ahead = [delta for delta in deltas if delta >= 0]
        reach = rows * len(ahead)
        gap = spread(ahead, 2)
        mine = (gap >= 0) & (gap < per_dev)
        prompt = []
        for c in range(n_prompt // HD):
            sp = nt(q[:reach], kb[pl.ds(n_own + c * HD, HD), :])
            prompt.append(jnp.where(mine, sp, NEG))

        def join(head, tail):
            return jnp.concatenate([head, tail[reach:]], axis=0) if reach < tail.shape[0] else head

        top = join(functools.reduce(jnp.maximum, prompt, s[:reach]), s)
        m = jnp.max(top, axis=1, keepdims=True)
        if fresh is not None:
            m = jnp.maximum(m, fresh)
        p = jnp.exp((s - m) * scale)
        weights = [jnp.exp((sp - m[:reach]) * scale).astype(jnp.bfloat16) for sp in prompt]
        kept = p.astype(jnp.bfloat16).astype(jnp.float32)
        total = functools.reduce(
            jnp.add, [x.astype(jnp.float32) for x in weights], kept[:reach]
        )
        total = jnp.sum(join(total, kept), axis=1, keepdims=True)
        picked = [jnp.where(rel == c, p, 0.0).astype(jnp.bfloat16) for c in range(per_dev)]
        w = jnp.dot(
            jnp.concatenate(picked, axis=1), vb[pl.ds(0, n_own), :],
            preferred_element_type=jnp.float32,
        )
        w_prompt = jnp.dot(
            jnp.concatenate(weights, axis=1), vb[pl.ds(n_own, n_prompt), :],
            preferred_element_type=jnp.float32,
        )
        w = join(w[:reach] + w_prompt, w)
        return m, total, w

    k_tiled = jnp.concatenate([new_k] * groups, axis=0)
    v_tiled = jnp.concatenate([new_v] * groups, axis=0)
    fresh = jnp.sum(qrows * k_tiled, axis=1, keepdims=True)
    m0, l0, w0 = attend(qs[...], (0,), fresh)
    pf = jnp.exp((fresh - m0) * scale)
    l0 = l0 + pf
    w0 = w0 + pf * v_tiled

    for k, delta in enumerate(NEAR):
        @pl.when(there(delta))
        def _():
            q_copy(k, d + delta).wait_recv()
    m, total, w = attend(qin[...], NEAR)
    lanes = lax.broadcasted_iota(jnp.int32, w.shape, 1)
    stats = jnp.zeros(w.shape, jnp.float32)
    at = 0
    for value, count in ((m, 3), (total, 2)):
        left = value
        for _ in range(count):
            piece = left.astype(jnp.bfloat16).astype(jnp.float32)
            left = left - piece
            stats = jnp.where(lanes == at, piece, stats)
            at += 1
    for k, delta in enumerate(NEAR):
        res[k, :, pl.ds(0, HD)] = w[k * rows:(k + 1) * rows].astype(jnp.bfloat16)
        res[k, :, pl.ds(HD, HD)] = stats[k * rows:(k + 1) * rows].astype(jnp.bfloat16)
        @pl.when(there(delta))
        def _():
            r_copy(k, NEAR.index(-delta), d + delta).start()

    parts = [(m0, l0, w0)]
    for k, delta in enumerate(NEAR):
        @pl.when(there(delta))
        def _():
            r_copy(k, k, d + delta).wait_recv()
        w = rin[k, :, pl.ds(0, HD)].astype(jnp.float32)
        st = rin[k, :, pl.ds(HD, HD)].astype(jnp.float32)
        m = st[:, 0:1] + st[:, 1:2] + st[:, 2:3]
        l = st[:, 3:4] + st[:, 4:5]
        m = jnp.where(there(delta), m, NEG)
        parts.append((m, l, w))
    peak = functools.reduce(jnp.maximum, [x[0] for x in parts])
    weighted = jnp.zeros((rows, HD), jnp.float32)
    total = jnp.zeros((rows, 1), jnp.float32)
    for m, l, w in parts:
        f = jnp.exp((m - peak) * scale)
        weighted = weighted + w * f
        total = total + l * f
    att = weighted / total
    att = jnp.concatenate(
        [att[g * per_dev:(g + 1) * per_dev] for g in range(groups)], axis=1
    ).astype(jnp.bfloat16)

    w_load.wait()
    width = w_hbm.shape[1] // n_tp

    def o_copy(j):
        return pltpu.make_async_remote_copy(
            src_ref=part.at[j - 1],
            dst_ref=pin.at[j - 1],
            send_sem=o_send.at[j - 1],
            recv_sem=o_recv.at[j - 1],
            device_id={"tp": lax.rem(t + j, n_tp)},
            device_id_type=MESH,
        )

    def project(j):
        start = pl.multiple_of(lax.rem(t + j, n_tp) * width, width)
        y = jnp.dot(att, wv[:, pl.ds(start, width)], preferred_element_type=jnp.float32)
        return jnp.concatenate([y[:, :width // 2], y[:, width // 2:]], axis=0)

    for j in range(n_tp - 1, 0, -1):
        part[j - 1] = project(j).astype(jnp.bfloat16)
        o_copy(j).start()
    y = project(0)
    for j in range(n_tp - 1, 0, -1):
        o_copy(j).wait_recv()
        y = y + pin[j - 1].astype(jnp.float32)
    y = jnp.concatenate([y[:per_dev], y[per_dev:]], axis=1)
    out_ref[...] = y.astype(jnp.bfloat16)

    for k, delta in enumerate(NEAR):
        @pl.when(there(delta))
        def _():
            q_copy(NEAR.index(-delta), d + delta).wait_send()
            r_copy(k, NEAR.index(-delta), d + delta).wait_send()
    for j in range(1, n_tp):
        o_copy(j).wait_send()


def local(n, n_tp, queries, new_kv, own_kv, prompt_kv, out_weight, parents, own_len, first_beam):
    per_dev, q_width = queries.shape
    rows = per_dev * q_width // HD
    own = own_kv.reshape(-1, HD)
    prompt = prompt_kv.reshape(-1, HD)
    new = new_kv.reshape(-1, HD)
    total = own.shape[0] + prompt.shape[0]
    width = out_weight.shape[1] // n_tp
    vmem = pl.BlockSpec(memory_space=pltpu.VMEM)
    smem = pl.BlockSpec(memory_space=pltpu.SMEM)
    hbm = pl.BlockSpec(memory_space=pl.ANY)
    near = len(NEAR)
    bf16, f32 = jnp.bfloat16, jnp.float32
    dma = pltpu.SemaphoreType.DMA
    return pl.pallas_call(
        functools.partial(kernel, n, n_tp),
        out_shape=jax.ShapeDtypeStruct((per_dev, width), bf16),
        in_specs=[vmem, vmem, hbm, hbm, hbm, smem, smem, smem],
        out_specs=vmem,
        scratch_shapes=[
            pltpu.VMEM((rows, HD), bf16),
            pltpu.VMEM((near * rows, HD), bf16),
            pltpu.VMEM((total, HD), bf16),
            pltpu.VMEM((total, HD), f32),
            pltpu.VMEM(new.shape, f32),
            pltpu.VMEM((total // 2, HD), bf16),
            pltpu.VMEM((total // 2, HD), bf16),
            pltpu.VMEM(out_weight.shape, bf16),
            pltpu.VMEM((near, rows, 2 * HD), bf16),
            pltpu.VMEM((near, rows, 2 * HD), bf16),
            pltpu.VMEM((n_tp - 1, 2 * per_dev, width // 2), bf16),
            pltpu.VMEM((n_tp - 1, 2 * per_dev, width // 2), bf16),
            dma((3,)),
            dma((near,)),
            dma((near,)),
            dma((near,)),
            dma((near,)),
            dma((n_tp - 1,)),
            dma((n_tp - 1,)),
        ],
        compiler_params=pltpu.CompilerParams(
            collective_id=0, has_side_effects=True, vmem_limit_bytes=58 * 1024 * 1024
        ),
    )(queries, new, own, prompt, out_weight, parents, own_len, first_beam)


def solution(mesh):
    in_specs = (
        P("req", "tp"),
        P("req", None, "tp"),
        P("req", None, None, "tp"),
        P("req", None, None, "tp"),
        P("tp", None),
        P(),
        P(),
        P(),
    )
    out_specs = P("req", "tp")
    run = functools.partial(local, mesh.shape["req"], mesh.shape["tp"])
    return jax.shard_map(run, mesh=mesh, in_specs=in_specs, out_specs=out_specs, check_vma=False)
```

```python
import functools

import jax
import jax.numpy as jnp
from jax import lax
from jax.experimental import pallas as pl
from jax.experimental.pallas import tpu as pltpu
from jax.sharding import PartitionSpec as P

HD = 128
MOST_BEAMS = 16
NEG = -1e30
MESH = pl.DeviceIdType.MESH

NEAR = (1, 2, -1, -2)


def nt(a, b):
    return lax.dot_general(
        a, b, (((1,), (1,)), ((), ())), preferred_element_type=jnp.float32
    )


def eye(count):
    i = lax.broadcasted_iota(jnp.int32, (count, HD), 0)
    j = lax.broadcasted_iota(jnp.int32, (count, HD), 1)
    return jnp.where(i == j, 1.0, 0.0).astype(jnp.bfloat16)


def kernel(
    n, n_tp,
    q_ref, new_ref, own_hbm, prompt_hbm, w_hbm, parents, own_len, first_beam,
    out_ref,
    qs, qin, kvb, kvf, newf, kb, vb, wv, res, rin, part, pin,
    load_sem, q_send, q_recv, r_send, r_recv, o_send, o_recv,
):
    per_dev = q_ref.shape[0]
    groups = q_ref.shape[1] // HD
    rows = per_dev * groups
    own_rows, prompt_rows = own_hbm.shape[0], prompt_hbm.shape[0]
    n_own, n_prompt = own_rows // 2, prompt_rows // 2
    n_keys = n_own + n_prompt
    cache = n_own // per_dev
    scale = HD ** -0.5
    d = lax.axis_index("req")
    t = lax.axis_index("tp")

    def there(delta):
        return d + delta < n if delta > 0 else d + delta >= 0

    own_load = pltpu.make_async_copy(own_hbm, kvb.at[pl.ds(0, own_rows)], load_sem.at[0])
    prompt_load = pltpu.make_async_copy(
        prompt_hbm, kvb.at[pl.ds(own_rows, prompt_rows)], load_sem.at[1]
    )
    w_load = pltpu.make_async_copy(w_hbm, wv, load_sem.at[2])

    barrier = pltpu.get_barrier_semaphore()
    for delta in NEAR:
        @pl.when(there(delta))
        def _():
            pl.semaphore_signal(
                barrier, inc=1, device_id={"req": d + delta}, device_id_type=MESH
            )
    for j in range(1, n_tp):
        pl.semaphore_signal(
            barrier, inc=1, device_id={"tp": lax.rem(t + j, n_tp)}, device_id_type=MESH
        )
    own_load.start()
    prompt_load.start()
    w_load.start()

    qf = q_ref[...].astype(jnp.float32)
    qrows = jnp.concatenate([qf[:, g * HD:(g + 1) * HD] for g in range(groups)], axis=0)
    qs[...] = qrows.astype(jnp.bfloat16)

    for k, delta in enumerate(NEAR):
        @pl.when(jnp.logical_not(there(delta)))
        def _():
            qin[pl.ds(k * rows, rows), :] = jnp.zeros((rows, HD), jnp.bfloat16)
            rin[k] = jnp.zeros(rin.shape[1:], jnp.bfloat16)

    peers = n_tp - 1
    for delta in NEAR:
        peers = peers + jnp.where(there(delta), 1, 0)
    pl.semaphore_wait(barrier, peers)

    def q_copy(k, target):
        return pltpu.make_async_remote_copy(
            src_ref=qs,
            dst_ref=qin.at[pl.ds(k * rows, rows)],
            send_sem=q_send.at[k],
            recv_sem=q_recv.at[k],
            device_id={"req": target},
            device_id_type=MESH,
        )

    def r_copy(k_from, k_to, target):
        return pltpu.make_async_remote_copy(
            src_ref=res.at[k_from],
            dst_ref=rin.at[k_to],
            send_sem=r_send.at[k_to],
            recv_sem=r_recv.at[k_to],
            device_id={"req": target},
            device_id_type=MESH,
        )

    for delta in NEAR:
        @pl.when(there(delta))
        def _():
            q_copy(NEAR.index(-delta), d + delta).start()

    sub = lax.broadcasted_iota(jnp.int32, (per_dev, HD), 0)
    lane = lax.broadcasted_iota(jnp.int32, (per_dev, HD), 1)

    def beam_facts(delta):
        source = lax.rem(d + delta + n, n)
        rel = jnp.zeros((per_dev, HD), jnp.int32)
        length = jnp.zeros((per_dev, HD), jnp.int32)
        gap = jnp.zeros((per_dev, HD), jnp.int32)
        for i in range(per_dev):
            b = source * per_dev + i
            parent = parents[b]
            here = sub == i
            rel = jnp.where(here, parent - d * per_dev, rel)
            length = jnp.where(here, own_len[parent], length)
            if delta >= 0:
                gap = jnp.where(here, first_beam[b] - d * per_dev, gap)
        return rel, length, gap

    facts = {delta: beam_facts(delta) for delta in (0,) + NEAR}

    def spread(deltas, which):
        return jnp.concatenate(
            [facts[delta][which] for delta in deltas for _ in range(groups)], axis=0
        )

    newf[...] = new_ref[...].astype(jnp.float32)
    new_k = newf[pl.ds(0, per_dev, stride=2), :]
    new_v = newf[pl.ds(1, per_dev, stride=2), :]

    own_load.wait()
    kvf[pl.ds(0, own_rows), :] = kvb[pl.ds(0, own_rows), :].astype(jnp.float32)
    prompt_load.wait()
    kvf[pl.ds(own_rows, prompt_rows), :] = kvb[pl.ds(own_rows, prompt_rows), :].astype(jnp.float32)
    kb[...] = kvf[pl.ds(0, n_keys, stride=2), :].astype(jnp.bfloat16)
    vb[...] = kvf[pl.ds(1, n_keys, stride=2), :].astype(jnp.bfloat16)

    def attend(q, deltas, fresh=None):
        rel = spread(deltas, 0)
        length = spread(deltas, 1)
        lanes = lax.broadcasted_iota(jnp.int32, rel.shape, 1)
        s = jnp.full(rel.shape, NEG, jnp.float32)
        for c in range(per_dev):
            s = jnp.where(rel == c, nt(q, kb[pl.ds(c * cache, cache), :]), s)
        s = jnp.where(lanes < length, s, NEG)
        ahead = [delta for delta in deltas if delta >= 0]
        reach = rows * len(ahead)
        gap = spread(ahead, 2)
        mine = (gap >= 0) & (gap < per_dev)
        prompt = []
        for c in range(n_prompt // HD):
            sp = nt(q[:reach], kb[pl.ds(n_own + c * HD, HD), :])
            prompt.append(jnp.where(mine, sp, NEG))

        def join(head, tail):
            return jnp.concatenate([head, tail[reach:]], axis=0) if reach < tail.shape[0] else head

        top = join(functools.reduce(jnp.maximum, prompt, s[:reach]), s)
        m = jnp.max(top, axis=1, keepdims=True)
        if fresh is not None:
            m = jnp.maximum(m, fresh)
        p = jnp.exp((s - m) * scale)
        weights = [jnp.exp((sp - m[:reach]) * scale).astype(jnp.bfloat16) for sp in prompt]
        kept = p.astype(jnp.bfloat16).astype(jnp.float32)
        total = functools.reduce(
            jnp.add, [x.astype(jnp.float32) for x in weights], kept[:reach]
        )
        total = jnp.sum(join(total, kept), axis=1, keepdims=True)
        picked = [jnp.where(rel == c, p, 0.0).astype(jnp.bfloat16) for c in range(per_dev)]
        w = jnp.dot(
            jnp.concatenate(picked, axis=1), vb[pl.ds(0, n_own), :],
            preferred_element_type=jnp.float32,
        )
        w_prompt = jnp.dot(
            jnp.concatenate(weights, axis=1), vb[pl.ds(n_own, n_prompt), :],
            preferred_element_type=jnp.float32,
        )
        w = join(w[:reach] + w_prompt, w)
        return m, total, w

    k_tiled = jnp.concatenate([new_k] * groups, axis=0)
    v_tiled = jnp.concatenate([new_v] * groups, axis=0)
    fresh = jnp.sum(qrows * k_tiled, axis=1, keepdims=True)
    m0, l0, w0 = attend(qs[...], (0,), fresh)
    pf = jnp.exp((fresh - m0) * scale)
    l0 = l0 + pf
    w0 = w0 + pf * v_tiled

    for k, delta in enumerate(NEAR):
        @pl.when(there(delta))
        def _():
            q_copy(k, d + delta).wait_recv()
    m, total, w = attend(qin[...], NEAR)
    lanes = lax.broadcasted_iota(jnp.int32, w.shape, 1)
    stats = jnp.zeros(w.shape, jnp.float32)
    at = 0
    for value, count in ((m, 3), (total, 2)):
        left = value
        for _ in range(count):
            piece = left.astype(jnp.bfloat16).astype(jnp.float32)
            left = left - piece
            stats = jnp.where(lanes == at, piece, stats)
            at += 1
    for k, delta in enumerate(NEAR):
        res[k, pl.ds(0, rows), :] = w[k * rows:(k + 1) * rows].astype(jnp.bfloat16)
        flipped = lax.dot_general(
            stats[k * rows:(k + 1) * rows].astype(jnp.bfloat16), eye(rows),
            (((0,), (0,)), ((), ())), preferred_element_type=jnp.float32,
        )
        res[k, pl.ds(rows, 16), :] = flipped[:16].astype(jnp.bfloat16)
        @pl.when(there(delta))
        def _():
            r_copy(k, NEAR.index(-delta), d + delta).start()

    parts = [(m0, l0, w0)]
    for k, delta in enumerate(NEAR):
        @pl.when(there(delta))
        def _():
            r_copy(k, k, d + delta).wait_recv()
        w = rin[k, pl.ds(0, rows), :].astype(jnp.float32)
        st = lax.dot_general(
            rin[k, pl.ds(rows, 16), :], eye(16),
            (((0,), (0,)), ((), ())), preferred_element_type=jnp.float32,
        )[:rows]
        m = st[:, 0:1] + st[:, 1:2] + st[:, 2:3]
        l = st[:, 3:4] + st[:, 4:5]
        m = jnp.where(there(delta), m, NEG)
        parts.append((m, l, w))
    peak = functools.reduce(jnp.maximum, [x[0] for x in parts])
    weighted = jnp.zeros((rows, HD), jnp.float32)
    total = jnp.zeros((rows, 1), jnp.float32)
    for m, l, w in parts:
        f = jnp.exp((m - peak) * scale)
        weighted = weighted + w * f
        total = total + l * f
    att = weighted / total
    att = jnp.concatenate(
        [att[g * per_dev:(g + 1) * per_dev] for g in range(groups)], axis=1
    ).astype(jnp.bfloat16)

    w_load.wait()
    width = w_hbm.shape[1] // n_tp

    def o_copy(j):
        return pltpu.make_async_remote_copy(
            src_ref=part.at[j - 1],
            dst_ref=pin.at[j - 1],
            send_sem=o_send.at[j - 1],
            recv_sem=o_recv.at[j - 1],
            device_id={"tp": lax.rem(t + j, n_tp)},
            device_id_type=MESH,
        )

    def project(j):
        start = pl.multiple_of(lax.rem(t + j, n_tp) * width, width)
        y = jnp.dot(att, wv[:, pl.ds(start, width)], preferred_element_type=jnp.float32)
        return jnp.concatenate([y[:, :width // 2], y[:, width // 2:]], axis=0)

    for j in range(n_tp - 1, 0, -1):
        part[j - 1] = project(j).astype(jnp.bfloat16)
        o_copy(j).start()
    y = project(0)
    for j in range(n_tp - 1, 0, -1):
        o_copy(j).wait_recv()
        y = y + pin[j - 1].astype(jnp.float32)
    y = jnp.concatenate([y[:per_dev], y[per_dev:]], axis=1)
    out_ref[...] = y.astype(jnp.bfloat16)

    for k, delta in enumerate(NEAR):
        @pl.when(there(delta))
        def _():
            q_copy(NEAR.index(-delta), d + delta).wait_send()
            r_copy(k, NEAR.index(-delta), d + delta).wait_send()
    for j in range(1, n_tp):
        o_copy(j).wait_send()


def local(n, n_tp, queries, new_kv, own_kv, prompt_kv, out_weight, parents, own_len, first_beam):
    per_dev, q_width = queries.shape
    rows = per_dev * q_width // HD
    own = own_kv.reshape(-1, HD)
    prompt = prompt_kv.reshape(-1, HD)
    new = new_kv.reshape(-1, HD)
    total = own.shape[0] + prompt.shape[0]
    width = out_weight.shape[1] // n_tp
    vmem = pl.BlockSpec(memory_space=pltpu.VMEM)
    smem = pl.BlockSpec(memory_space=pltpu.SMEM)
    hbm = pl.BlockSpec(memory_space=pl.ANY)
    near = len(NEAR)
    bf16, f32 = jnp.bfloat16, jnp.float32
    dma = pltpu.SemaphoreType.DMA
    return pl.pallas_call(
        functools.partial(kernel, n, n_tp),
        out_shape=jax.ShapeDtypeStruct((per_dev, width), bf16),
        in_specs=[vmem, vmem, hbm, hbm, hbm, smem, smem, smem],
        out_specs=vmem,
        scratch_shapes=[
            pltpu.VMEM((rows, HD), bf16),
            pltpu.VMEM((near * rows, HD), bf16),
            pltpu.VMEM((total, HD), bf16),
            pltpu.VMEM((total, HD), f32),
            pltpu.VMEM(new.shape, f32),
            pltpu.VMEM((total // 2, HD), bf16),
            pltpu.VMEM((total // 2, HD), bf16),
            pltpu.VMEM(out_weight.shape, bf16),
            pltpu.VMEM((near, rows + 16, HD), bf16),
            pltpu.VMEM((near, rows + 16, HD), bf16),
            pltpu.VMEM((n_tp - 1, 2 * per_dev, width // 2), bf16),
            pltpu.VMEM((n_tp - 1, 2 * per_dev, width // 2), bf16),
            dma((3,)),
            dma((near,)),
            dma((near,)),
            dma((near,)),
            dma((near,)),
            dma((n_tp - 1,)),
            dma((n_tp - 1,)),
        ],
        compiler_params=pltpu.CompilerParams(
            collective_id=0, has_side_effects=True, vmem_limit_bytes=58 * 1024 * 1024
        ),
    )(queries, new, own, prompt, out_weight, parents, own_len, first_beam)


def solution(mesh):
    in_specs = (
        P("req", "tp"),
        P("req", None, "tp"),
        P("req", None, None, "tp"),
        P("req", None, None, "tp"),
        P("tp", None),
        P(),
        P(),
        P(),
    )
    out_specs = P("req", "tp")
    run = functools.partial(local, mesh.shape["req"], mesh.shape["tp"])
    return jax.shard_map(run, mesh=mesh, in_specs=in_specs, out_specs=out_specs, check_vma=False)
```
